32 devices in a mesh: region: 4 (over z), tile: 8 (over y, x, core).
Axes of the slice: x: 2, y: 2, z: 4, core: 2. Of those that a mesh axis runs over, the one named last changes fastest.
Arguments:
- values: bfloat16 [131072, 256], P(('region', 'tile')), may hold values from -6 to 6
- halo_rows: int32 [2, 8192], P(None, ('region', 'tile')), may hold values from 0 to 4095
- neighbors: int32 [6, 131072], P(None, ('region', 'tile')), may hold values from 0 to 4607
- grad_weights: float32 [2, 6, 131072], P(None, None, ('region', 'tile')), may hold values from -2.5 to 2.5
- face_offsets: float32 [2, 6, 131072], P(None, None, ('region', 'tile')), may hold values from -3 to 3
- send_rows: int32 [32, 6144], P(('region', 'tile')), may hold values from 0 to 4095
- margin_slot: int32 [4096, 128], P(('region', 'tile')), may hold values from 0 to 6143, as said below
- margin_cell: int32 [4096, 128], P(('region', 'tile')), may hold values from 0 to 31, as said below
- margin_count: int32 [4096], P(('region', 'tile')), may hold values from 64 to 128, as said below
- margin_area: float32 [4096, 128], P(('region', 'tile')), may hold values from 0.05 to 1
- margin_offset: float32 [2, 4096, 128], P(None, ('region', 'tile')), may hold values from -3 to 3
Outputs:
- target_values: float32 [131072, 256], P(('region', 'tile'))
The draws below stay inside these ranges and needn't reach their ends.
Inputs may be any that keep to these rules, and one draw needn't show every extreme that they name: `margin_slot`: A tile's margins name rows only from source devices of its own region and of the two neighbouring regions, most of them from its own region. From each such source device only rows below some count are named; every device has some source device with its row 255 named. `margin_cell`: each of a tile's 32 cells is named by one of the tile's first 32 margins. `margin_count`: every device has a tile with all 128 margins live.
All inputs are finite; a program needn't handle non-finite values.
Results may differ from the reference program's by a relative error of at most 0.0011.
Values may be sent and summed in bfloat16 or wider, within the bound.
A program may use at most 64 MiB of HBM per device.

```python
import math
import jax
import jax.numpy as jnp
from jax import lax

SC = 4096
TT = 32
OV = 128
CH = 256
HS = 256
RS = 256
NT = 128
CELLS = 131072
TILES = 4096
N_REGION = 4
N_TILE = 8


def draw_margin_slot(key, part):
    key = jax.random.fold_in(key, 11)
    key_count, key_offset, key_side, key_tile, key_row = jax.random.split(key, 5)
    devices = TILES // NT
    pairs = 3 * N_TILE
    counts = jax.random.randint(key_count, (devices, pairs), 1, RS + 1)
    offset = jax.random.randint(key_offset, (), 0, pairs)
    full_pair = (jnp.arange(devices, dtype=jnp.int32) + offset) % pairs
    counts = jnp.where(jnp.arange(pairs, dtype=jnp.int32)[None, :] == full_pair[:, None], RS, counts)
    side_draw = jax.random.randint(key_side, (devices, NT * OV), 0, 5)
    side = jnp.where(side_draw == 0, 0, jnp.where(side_draw == 4, 2, 1))
    tile_pick = jax.random.randint(key_tile, (devices, NT * OV), 0, N_TILE)
    pair = side * N_TILE + tile_pick
    row_limit = jnp.take_along_axis(counts, pair, axis=1)
    row_pick = jax.random.randint(key_row, (devices, NT * OV), 0, row_limit)
    slot_ids = pair * RS + row_pick
    slot_ids = slot_ids.at[:, 0].set(full_pair * RS + RS - 1)
    return slot_ids.reshape(TILES, OV).astype(jnp.int32)


def draw_margin_cell(key, part):
    key = jax.random.fold_in(key, 12)
    key_rotate, key_rest = jax.random.split(key, 2)
    rotate_by = jax.random.randint(key_rotate, (TILES, 1), 0, TT)
    leading = (jnp.arange(TT, dtype=jnp.int32)[None, :] + rotate_by) % TT
    trailing = jax.random.randint(key_rest, (TILES, OV - TT), 0, TT)
    return jnp.concatenate([leading, trailing], axis=1).astype(jnp.int32)


def draw_margin_count(key, part):
    key = jax.random.fold_in(key, 13)
    key_count, key_full = jax.random.split(key, 2)
    devices = TILES // NT
    counts = jax.random.randint(key_count, (devices, NT), OV // 2, OV + 1)
    full_tile = jax.random.randint(key_full, (devices, 1), 0, NT)
    counts = jnp.where(jnp.arange(NT, dtype=jnp.int32)[None, :] == full_tile, OV, counts)
    return counts.reshape(TILES).astype(jnp.int32)


def plant(entries, rng, low, high):
    index_at = [jax.random.randint(jax.random.fold_in(rng, axis), (), 0, length) for axis, length in enumerate(entries.shape)]
    widest = entries.shape.index(max(entries.shape))
    beside = index_at[:widest] + [(index_at[widest] + 1) % entries.shape[widest]] + index_at[widest + 1:]
    return entries.at[tuple(index_at)].set(low).at[tuple(beside)].set(high)


def steps_of(key, shape, shards, smallest, largest):
    level = 1.0
    for position, parts in shards:
        steps = jax.random.uniform(jax.random.fold_in(jax.random.fold_in(key, 6), position), (parts,), jnp.float32, smallest / len(shards), largest / len(shards))
        level = level * jnp.repeat(jnp.exp(steps), shape[position] // parts).reshape((-1,) + (1,) * (len(shape) - 1 - position))
    return level


def gaussian(own_key, extent, spread, bound, cuts=(), held_as=jnp.bfloat16):
    factor_of = steps_of(own_key, extent, cuts, -0.22, 0.18) if cuts else 1.0
    values = jax.random.normal(own_key, extent, jnp.float32) * spread * factor_of
    return jnp.minimum(jnp.maximum(values, -bound), bound).astype(held_as)


def setup_inputs(seed: int = 0) -> dict:
    key_of = jax.random.split(jax.random.key(seed), 12)
    return {
        "values": gaussian(key_of[0], (CELLS, CH), 1.0, 6.0, ((0, 32),)),
        "halo_rows": plant(jax.random.randint(key_of[1], (2, N_REGION * N_TILE * HS), 0, SC), jax.random.fold_in(key_of[1], 1), 0, SC - 1).astype(jnp.int32),
        "neighbors": plant(jax.random.randint(key_of[2], (6, CELLS), 0, SC + 2 * HS), jax.random.fold_in(key_of[2], 1), 0, (SC + 2 * HS) - 1).astype(jnp.int32),
        "grad_weights": gaussian(key_of[3], (2, 6, CELLS), 6 ** -0.5, 2.5, ((2, 32),), jnp.float32),
        "face_offsets": gaussian(key_of[4], (2, 6, CELLS), 0.5, 3.0, ((2, 32),), jnp.float32),
        "send_rows": plant(jax.random.randint(key_of[5], (N_REGION * N_TILE, 3 * N_TILE * RS), 0, SC), jax.random.fold_in(key_of[5], 1), 0, SC - 1).astype(jnp.int32),
        "margin_slot": draw_margin_slot(jax.random.fold_in(key_of[11], 71), 0),
        "margin_cell": draw_margin_cell(jax.random.fold_in(key_of[11], 71), 0),
        "margin_count": draw_margin_count(jax.random.fold_in(key_of[11], 71), 0),
        "margin_area": jnp.clip(jnp.exp(math.log(1.0) - 2.9957323 * jax.random.uniform(key_of[9], (TILES, OV), jnp.float32) ** steps_of(key_of[9], (TILES, OV), ((0, 32),), -0.2, 0.2)), 0.05, 1.0),
        "margin_offset": gaussian(key_of[10], (2, TILES, OV), 0.5, 3.0, ((1, 32),), jnp.float32),
    }


venkat_eps = 0.04


def limited_rows(values_own, extended, neighbor_ids, weighting, face_geom):
    center = values_own.astype(jnp.float32)
    cell_count = center.shape[0]
    stacked = jnp.take(extended, neighbor_ids.reshape(-1), axis=0, mode="clip").reshape(
        6, cell_count, center.shape[1])
    grad_x = jnp.zeros(center.shape, jnp.float32)
    grad_y = jnp.zeros(center.shape, jnp.float32)
    upper_val = center
    lower_val = center
    for face_num in range(6):
        beside = stacked[face_num].astype(jnp.float32)
        difference = beside - center
        grad_x = grad_x + weighting[0, face_num][:, None] * difference
        grad_y = grad_y + weighting[1, face_num][:, None] * difference
        upper_val = jnp.maximum(upper_val, beside)
        lower_val = jnp.minimum(lower_val, beside)
    headroom = upper_val - center
    footroom = center - lower_val
    limiter = jnp.ones(center.shape, jnp.float32)
    for face_num in range(6):
        face_delta = grad_x * face_geom[0, face_num][:, None] + grad_y * face_geom[1, face_num][:, None]
        face_bound = jnp.where(face_delta > 0, headroom, -footroom)
        venkat_ratio = (face_bound * face_bound + venkat_eps + 2.0 * face_delta * face_bound) / (
            face_bound * face_bound + 2.0 * face_delta * face_delta + face_delta * face_bound + venkat_eps)
        limiter = jnp.minimum(limiter, venkat_ratio)
    return jnp.concatenate([values_own, (limiter * grad_x).astype(jnp.bfloat16),
                            (limiter * grad_y).astype(jnp.bfloat16)], axis=1)


def remap_tiles(arrived, slot_ids, cell_ids, weighting, offset_x, offset_y):
    row_data = jnp.take(arrived, slot_ids.reshape(-1), axis=0, mode="clip").reshape(
        slot_ids.shape + (arrived.shape[1],)).astype(jnp.float32)
    chan_width = row_data.shape[2] // 3
    phi_part = row_data[..., :chan_width]
    slope_x = row_data[..., chan_width:2 * chan_width]
    slope_y = row_data[..., 2 * chan_width:]
    contribution = weighting[..., None] * (phi_part + offset_x[..., None] * slope_x + offset_y[..., None] * slope_y)
    one_hot = (cell_ids[:, None, :] == lax.broadcasted_iota(jnp.int32, (1, TT, 1), 1)).astype(contribution.dtype)
    summed = jnp.einsum('gto,goc->gtc', one_hot, contribution, precision=lax.Precision.HIGHEST)
    area_sum = jnp.einsum('gto,go->gt', one_hot, weighting, precision=lax.Precision.HIGHEST)
    return (summed / area_sum[..., None]).reshape(-1, chan_width)


def reference(values, halo_rows, neighbors, grad_weights, face_offsets, send_rows, margin_slot, margin_cell,
              margin_count, margin_area, margin_offset):
    devices = N_REGION * N_TILE
    blocks = values.reshape(devices, SC, CH)
    halo_blocks = halo_rows.reshape(2, devices, HS)
    neighbor_blocks = jnp.transpose(neighbors.reshape(6, devices, SC), (1, 0, 2))
    weight_blocks = jnp.transpose(grad_weights.reshape(2, 6, devices, SC), (2, 0, 1, 3))
    geom_blocks = jnp.transpose(face_offsets.reshape(2, 6, devices, SC), (2, 0, 1, 3))

    def source_side(pieces):
        dev_id, neighbor_ids, weighting, face_geom = pieces
        previous = (dev_id + devices - 1) % devices
        following = (dev_id + 1) % devices
        from_before = blocks[previous][halo_blocks[1, previous]]
        from_after = blocks[following][halo_blocks[0, following]]
        extended = jnp.concatenate([blocks[dev_id], from_before, from_after], axis=0)
        return limited_rows(blocks[dev_id], extended, neighbor_ids, weighting, face_geom)

    dev_ids = jnp.arange(devices, dtype=jnp.int32)
    recon = lax.map(source_side, (dev_ids, neighbor_blocks, weight_blocks, geom_blocks))
    send_blocks = send_rows.reshape(devices, 3, N_TILE, RS)
    is_live = lax.broadcasted_iota(jnp.int32, (TILES, OV), 1) < margin_count[:, None]
    weight = jnp.where(is_live, margin_area, jnp.zeros_like(margin_area))
    side_ids = jnp.arange(3, dtype=jnp.int32)
    tile_ids = jnp.arange(N_TILE, dtype=jnp.int32)

    def target_side(pieces):
        dev_id, slot_ids, cell_ids, weighting, offset_x, offset_y = pieces
        home_region = dev_id // N_TILE
        home_tile = dev_id % N_TILE
        src_region = (home_region - 1 + side_ids + N_REGION) % N_REGION
        src_dev = (src_region[:, None] * N_TILE + tile_ids[None, :]).astype(jnp.int32)
        chosen = send_blocks[src_dev, side_ids[:, None], home_tile]
        arrived = recon[src_dev[:, :, None], chosen].reshape(3 * N_TILE * RS, 3 * CH)
        return remap_tiles(arrived, slot_ids, cell_ids, weighting, offset_x, offset_y)

    mapped = lax.map(target_side, (dev_ids, margin_slot.reshape(devices, NT, OV),
                                   margin_cell.reshape(devices, NT, OV), weight.reshape(devices, NT, OV),
                                   margin_offset[0].reshape(devices, NT, OV),
                                   margin_offset[1].reshape(devices, NT, OV)))
    return mapped.reshape(TILES * TT, CH)
```

```python
import functools

import jax
import jax.numpy as jnp
from jax import lax
from jax.experimental import pallas as pl
from jax.experimental.pallas import tpu as pltpu
from jax.sharding import PartitionSpec as P

TT = 32
EPS = 0.04
MESH = pl.DeviceIdType.MESH
L = 128
VMEM_LIMIT = 60 * 1024 * 1024


def limit_block(center, beside, geom):
    grad_x = None
    upper = center
    lower = center
    for j in range(6):
        diff = beside[j] - center
        px = geom(j) * diff
        py = geom(6 + j) * diff
        grad_x = px if grad_x is None else grad_x + px
        grad_y = py if j == 0 else grad_y + py
        upper = jnp.maximum(upper, beside[j])
        lower = jnp.minimum(lower, beside[j])
    head = upper - center
    foot = lower - center
    head2 = head * head + EPS
    foot2 = foot * foot + EPS
    num = None
    for j in range(6):
        delta = grad_x * geom(12 + j) + grad_y * geom(18 + j)
        up = delta > 0
        bound = jnp.where(up, head, foot)
        s = jnp.where(up, head2, foot2)
        p = delta * bound
        sp = s + p
        n = sp + p
        d = sp + 2.0 * (delta * delta)
        if num is None:
            less = n < d
            num = jnp.where(less, n, 1.0)
            den = jnp.where(less, d, 1.0)
        else:
            less = n * den < num * d
            num = jnp.where(less, n, num)
            den = jnp.where(less, d, den)
    lim = num / den
    return lim * grad_x, lim * grad_y


def source_kernel(vals, halo, geom, nb, send, out, tab, nbuf, rec, pbuf):
    cells = vals.shape[0]
    extra = halo.shape[0]
    rows = out.shape[0]
    T = 32

    def fill(src, start):
        def body(c, carry):
            b = pl.multiple_of(c * T, T)
            x = src[pl.ds(b, T), :].astype(jnp.float32)
            for h in range(2):
                tab[pl.ds(2 * (start + b) + h, T, stride=2), :] = x[:, h * L : (h + 1) * L]
            return carry

        lax.fori_loop(0, src.shape[0] // T, body, 0)

    fill(vals, 0)
    fill(halo, cells)

    def body(c, carry):
        b = pl.multiple_of(c * T, T)
        for j in range(6):
            for u in range(T):
                i = pl.multiple_of(nb[j * cells + b + u], 2)
                nbuf[pl.ds(2 * (j * T + u), 2), :] = tab[pl.ds(i, 2), :]
        for s in range(T // 8):
            g = geom[pl.ds(b + 8 * s, 8), :]
            cols = [jnp.broadcast_to(g[:, m : m + 1], (8, L)) for m in range(24)]
            for h in range(2):
                center = tab[pl.ds(2 * b + 16 * s + h, 8, stride=2), :]
                beside = [nbuf[pl.ds(2 * (j * T + 8 * s) + h, 8, stride=2), :] for j in range(6)]
                gx, gy = limit_block(center, beside, lambda m: cols[m])
                r = 8 * b + 64 * s
                rec[pl.ds(r + h, 8, stride=8), :] = center
                rec[pl.ds(r + 2 + h, 8, stride=8), :] = gx
                rec[pl.ds(r + 4 + h, 8, stride=8), :] = gy
        return carry

    lax.fori_loop(0, cells // T, body, 0)

    def pack(c, carry):
        b = pl.multiple_of(c * T, T)
        for u in range(T):
            i = pl.multiple_of(send[b + u], 8)
            pbuf[pl.ds(8 * u, 8), :] = rec[pl.ds(i, 8), :]
        for q in range(6):
            out[pl.ds(b, T), q * L : (q + 1) * L] = pbuf[pl.ds(q, T, stride=8), :].astype(jnp.bfloat16)
        return carry

    lax.fori_loop(0, rows // T, pack, 0)


def exchange_kernel(regions, tiles, src, dst, send_sem, recv_sem, own_sem):
    g = lax.axis_index("region")
    k = lax.axis_index("tile")
    rows = src.shape[0] // (3 * tiles)

    barrier = pltpu.get_barrier_semaphore()
    count = 0
    for step in (-1, 0, 1):
        for d in range(tiles):
            if step == 0 and d == 0:
                continue
            where = (lax.rem(g + step + regions, regions), lax.rem(k + d, tiles))
            pl.semaphore_signal(barrier, inc=1, device_id=where, device_id_type=MESH)
            count += 1
    pl.semaphore_wait(barrier, count)

    def block(ref, e, j):
        return ref.at[pl.ds(pl.multiple_of((e * tiles + j) * rows, rows), rows), :]

    sends = []
    for d in range(tiles):
        for e in (0, 2, 1):
            j = lax.rem(k + d, tiles)
            if e == 1 and d == 0:
                continue
            copy = pltpu.make_async_remote_copy(
                src_ref=block(src, e, j),
                dst_ref=block(dst, e, k),
                send_sem=send_sem.at[e * tiles + j],
                recv_sem=recv_sem.at[e * tiles + k],
                device_id=(lax.rem(g + 1 - e + regions, regions), j),
                device_id_type=MESH,
            )
            copy.start()
            sends.append(copy)
    own = pltpu.make_async_copy(block(src, 1, k), block(dst, 1, k), own_sem)
    own.start()
    for d in range(tiles):
        for e in (0, 2, 1):
            j = lax.rem(k + tiles - d, tiles)
            if e == 1 and d == 0:
                continue
            pltpu.make_async_remote_copy(
                src_ref=block(src, e, j),
                dst_ref=block(dst, e, j),
                send_sem=send_sem.at[e * tiles + j],
                recv_sem=recv_sem.at[e * tiles + j],
                device_id=(lax.rem(g + 1 - e + regions, regions), j),
                device_id_type=MESH,
            ).wait_recv()
    for copy in sends:
        copy.wait_send()
    own.wait()


def margin_kernel(arrived, slot, cell, count, area, offset, out, tab, gbuf):
    rows = arrived.shape[0]
    tiles, margins = cell.shape
    T = 32

    def fill(c, carry):
        b = pl.multiple_of(c * T, T)
        for q in range(6):
            tab[pl.ds(8 * b + q, T, stride=8), :] = arrived[pl.ds(b, T), q * L : (q + 1) * L].astype(jnp.float32)
        return carry

    lax.fori_loop(0, rows // T, fill, 0)

    def body(n, carry):
        for u in range(margins):
            i = pl.multiple_of(slot[n * margins + u], 8)
            gbuf[pl.ds(8 * u, 8), :] = tab[pl.ds(i, 8), :]
        one = pl.ds(n, 1)
        lane = lax.broadcasted_iota(jnp.int32, (1, margins), 1)
        w = jnp.where(lane < count[n], area[one, :], 0.0)
        hit = lax.broadcasted_iota(jnp.int32, (TT, margins), 0) == cell[one, :]
        w = jnp.where(hit, w, 0.0)
        total = jnp.sum(w, axis=1, keepdims=True)
        acc = None
        for m, weight in enumerate((w, w * offset[0, one, :], w * offset[1, one, :])):
            high = weight.astype(jnp.bfloat16)
            low = (weight - high.astype(jnp.float32)).astype(jnp.bfloat16)
            lhs = jnp.concatenate([high, low], axis=0)
            rhs = jnp.concatenate(
                [gbuf[pl.ds(2 * m + h, margins, stride=8), :].astype(jnp.bfloat16) for h in range(2)], axis=1
            )
            part = jnp.dot(lhs, rhs, preferred_element_type=jnp.float32)
            acc = part if acc is None else acc + part
        out[pl.ds(pl.multiple_of(n * TT, TT), TT), :] = (acc[:TT] + acc[TT:]) / total
        return carry

    lax.fori_loop(0, tiles, body, 0)


def local(
    values,
    halo_rows,
    neighbors,
    grad_weights,
    face_offsets,
    send_rows,
    margin_slot,
    margin_cell,
    margin_count,
    margin_area,
    margin_offset,
):
    regions = lax.axis_size("region")
    tiles = lax.axis_size("tile")
    devices = regions * tiles
    cells, width = values.shape
    hs = halo_rows.shape[1]
    rows = send_rows.shape[1]
    tile_count, margins = margin_slot.shape
    listed = jnp.take(values, halo_rows.reshape(-1), axis=0, mode="clip")
    axes = ("region", "tile")
    before = lax.ppermute(listed[hs:], axes, [(i, (i + 1) % devices) for i in range(devices)])
    after = lax.ppermute(listed[:hs], axes, [((i + 1) % devices, i) for i in range(devices)])
    halo = jnp.concatenate([before, after], axis=0)
    geom = jnp.concatenate([grad_weights.reshape(12, cells), face_offsets.reshape(12, cells)], axis=0).T
    vmem = pl.BlockSpec(memory_space=pltpu.VMEM)
    smem = pl.BlockSpec(memory_space=pltpu.SMEM)
    hbm = pl.BlockSpec(memory_space=pl.ANY)
    outgoing = pl.pallas_call(
        source_kernel,
        out_shape=jax.ShapeDtypeStruct((rows, 3 * width), jnp.bfloat16),
        in_specs=[vmem, vmem, vmem, smem, smem],
        out_specs=vmem,
        scratch_shapes=[
            pltpu.VMEM((2 * (cells + 2 * hs), L), jnp.float32),
            pltpu.VMEM((2 * 6 * 32, L), jnp.float32),
            pltpu.VMEM((8 * cells, L), jnp.float32),
            pltpu.VMEM((8 * 32, L), jnp.float32),
        ],
        compiler_params=pltpu.CompilerParams(vmem_limit_bytes=VMEM_LIMIT),
        name="source_rows",
    )(values, halo, geom, (neighbors * 2).reshape(-1), (send_rows * 8).reshape(-1))
    arrived = pl.pallas_call(
        functools.partial(exchange_kernel, regions, tiles),
        out_shape=jax.ShapeDtypeStruct((rows, 3 * width), jnp.bfloat16),
        in_specs=[hbm],
        out_specs=hbm,
        scratch_shapes=[
            pltpu.SemaphoreType.DMA((3 * tiles,)),
            pltpu.SemaphoreType.DMA((3 * tiles,)),
            pltpu.SemaphoreType.DMA,
        ],
        compiler_params=pltpu.CompilerParams(collective_id=0, has_side_effects=True, vmem_limit_bytes=VMEM_LIMIT),
        name="exchange_rows",
    )(outgoing)
    return pl.pallas_call(
        margin_kernel,
        out_shape=jax.ShapeDtypeStruct((tile_count * TT, width), jnp.float32),
        in_specs=[vmem, smem, vmem, smem, vmem, vmem],
        out_specs=vmem,
        scratch_shapes=[
            pltpu.VMEM((8 * rows, L), jnp.float32),
            pltpu.VMEM((8 * margins, L), jnp.float32),
        ],
        compiler_params=pltpu.CompilerParams(vmem_limit_bytes=VMEM_LIMIT),
        name="margin_sums",
    )(arrived, (margin_slot * 8).reshape(-1), margin_cell, margin_count, margin_area, margin_offset)


def solution(mesh):
    return jax.shard_map(
        local,
        mesh=mesh,
        in_specs=(
            P(("region", "tile"), None),
            P(None, ("region", "tile")),
            P(None, ("region", "tile")),
            P(None, None, ("region", "tile")),
            P(None, None, ("region", "tile")),
            P(("region", "tile"), None),
            P(("region", "tile"), None),
            P(("region", "tile"), None),
            P(("region", "tile")),
            P(("region", "tile"), None),
            P(None, ("region", "tile"), None),
        ),
        out_specs=P(("region", "tile"), None),
        check_vma=False,
    )
```

```python
import functools

import jax
import jax.numpy as jnp
from jax import lax
from jax.experimental import pallas as pl
from jax.experimental.pallas import tpu as pltpu
from jax.sharding import PartitionSpec as P

TT = 32
EPS = 0.04
MESH = pl.DeviceIdType.MESH
L = 128
VMEM_LIMIT = 60 * 1024 * 1024


def limit_block(center, beside, geom):
    grad_x = None
    upper = center
    lower = center
    for j in range(6):
        diff = beside[j] - center
        px = geom(j) * diff
        py = geom(6 + j) * diff
        grad_x = px if grad_x is None else grad_x + px
        grad_y = py if j == 0 else grad_y + py
        upper = jnp.maximum(upper, beside[j])
        lower = jnp.minimum(lower, beside[j])
    head = upper - center
    foot = lower - center
    head2 = head * head + EPS
    foot2 = foot * foot + EPS
    num = None
    for j in range(6):
        delta = grad_x * geom(12 + j) + grad_y * geom(18 + j)
        up = delta > 0
        bound = jnp.where(up, head, foot)
        s = jnp.where(up, head2, foot2)
        p = delta * bound
        sp = s + p
        n = sp + p
        d = sp + 2.0 * (delta * delta)
        if num is None:
            less = n < d
            num = jnp.where(less, n, 1.0)
            den = jnp.where(less, d, 1.0)
        else:
            less = n * den < num * d
            num = jnp.where(less, n, num)
            den = jnp.where(less, d, den)
    lim = num / den
    return lim * grad_x, lim * grad_y


def loop(count, body):
    def step(c, carry):
        body(c)
        return carry

    lax.fori_loop(0, count, step, 0)


def unrolled(count, body):
    def step(c, carry):
        body(c)
        return carry

    lax.fori_loop(0, count, step, 0, unroll=True)


def remap_kernel(
    regions, tiles, vals, geom, nb, send, listed, slot, cell, count, area, offset, out,
    tab, nbuf, rec, pbuf, hsend, hrecv, s0, s1, s2, r0, r1, r2, mtab, gbuf,
    hsend_sem, hrecv_sem, send_sem, recv_sem,
):
    g = lax.axis_index("region")
    k = lax.axis_index("tile")
    devices = regions * tiles
    me = g * tiles + k
    cells = vals.shape[0]
    hs = hsend.shape[0] // 2
    rows = s0.shape[0] // (3 * tiles)
    tile_count, margins = cell.shape
    T = 32

    barrier = pltpu.get_barrier_semaphore()
    partners = 0
    for step in (-1, 0, 1):
        for d in range(tiles):
            if step == 0 and d == 0:
                continue
            where = (lax.rem(g + step + regions, regions), lax.rem(k + d, tiles))
            pl.semaphore_signal(barrier, inc=1, device_id=where, device_id_type=MESH)
            partners += 1

    def fill(src, start):
        def body(c):
            b = pl.multiple_of(c * T, T)
            x = src[pl.ds(b, T), :].astype(jnp.float32)
            for h in range(2):
                pbuf[pl.ds(h, T, stride=2), :] = x[:, h * L : (h + 1) * L]

            def one(u):
                tab[start + b + u] = pbuf[pl.ds(2 * u, 2), :]

            unrolled(T, one)

        loop(src.shape[0] // T, body)

    fill(vals, 0)
    pl.semaphore_wait(barrier, partners)

    def pack_values(index, src_row, dst, dst_row, n):
        def body(c):
            b = pl.multiple_of(c * T, T)

            def one(u):
                pbuf[pl.ds(2 * u, 2), :] = tab[index[src_row + b + u]]

            unrolled(T, one)
            at = pl.ds(pl.multiple_of(dst_row + b, T), T)
            for h in range(2):
                dst[at, h * L : (h + 1) * L] = pbuf[pl.ds(h, T, stride=2), :].astype(jnp.bfloat16)

        loop(n // T, body)

    pack_values(listed, 0, hsend, 0, 2 * hs)
    halo = []
    for part, step in ((1, 1), (0, devices - 1)):
        to = lax.rem(me + step, devices)
        copy = pltpu.make_async_remote_copy(
            src_ref=hsend.at[pl.ds(part * hs, hs), :],
            dst_ref=hrecv.at[pl.ds((1 - part) * hs, hs), :],
            send_sem=hsend_sem.at[part],
            recv_sem=hrecv_sem.at[part],
            device_id=(to // tiles, lax.rem(to, tiles)),
            device_id_type=MESH,
        )
        copy.start()
        halo.append(copy)

    def block_row(e, j):
        return pl.multiple_of((e * tiles + j) * rows, rows)

    def remote(p, src, dst, e, j, at):
        return pltpu.make_async_remote_copy(
            src_ref=src.at[pl.ds(block_row(e, j), rows), :],
            dst_ref=dst.at[pl.ds(block_row(e, at), rows), :],
            send_sem=send_sem.at[p * 3 * tiles + e * tiles + j],
            recv_sem=recv_sem.at[p * 3 * tiles + e * tiles + at],
            device_id=(lax.rem(g + 1 - e + regions, regions), j),
            device_id_type=MESH,
        )

    def each_block(body):
        def far(d):
            j = lax.rem(k + d, tiles)
            body(0, j)
            body(2, j)

        loop(tiles, far)
        loop(tiles - 1, lambda d: body(1, lax.rem(k + d + 1, tiles)))

    def receive(p, src, dst):
        def far(d):
            j = lax.rem(k + d, tiles)
            remote(p, src, dst, 0, j, j).wait_recv()
            remote(p, src, dst, 2, j, j).wait_recv()

        def near(d):
            j = lax.rem(k + d + 1, tiles)
            remote(p, src, dst, 1, j, j).wait_recv()

        loop(tiles, far)
        loop(tiles - 1, near)

    def send_values(e, j):
        row = block_row(e, j)
        pack_values(send, row, s0, row, rows)
        remote(0, s0, r0, e, j, k).start()

    each_block(send_values)
    pack_values(send, block_row(1, k), r0, block_row(1, k), rows)

    for copy in halo:
        copy.wait_recv()
    fill(hrecv, cells)

    def source(c):
        b = pl.multiple_of(c * T, T)
        for j in range(6):

            def one(u):
                nbuf[pl.ds(2 * (j * T + u), 2), :] = tab[nb[j * cells + b + u]]

            unrolled(T, one)
        mine = vals[pl.ds(b, T), :].astype(jnp.float32)
        for s in range(T // 8):
            w = geom[pl.ds(b + 8 * s, 8), :]
            cols = [jnp.broadcast_to(w[:, m : m + 1], (8, L)) for m in range(24)]
            for h in range(2):
                center = mine[8 * s : 8 * s + 8, h * L : (h + 1) * L]
                beside = [nbuf[pl.ds(2 * (j * T + 8 * s) + h, 8, stride=2), :] for j in range(6)]
                gx, gy = limit_block(center, beside, lambda m: cols[m])
                pbuf[pl.ds(32 * s + h, 8, stride=4), :] = gx
                pbuf[pl.ds(32 * s + 2 + h, 8, stride=4), :] = gy

        def keep(u):
            rec[b + u] = pbuf[pl.ds(4 * u, 4), :]

        unrolled(T, keep)

    loop(cells // T, source)

    def pack_slopes(src_row, to1, to2):
        def body(c):
            b = pl.multiple_of(c * T, T)

            def one(u):
                pbuf[pl.ds(4 * u, 4), :] = rec[send[src_row + b + u]]

            unrolled(T, one)
            at = pl.ds(pl.multiple_of(src_row + b, T), T)
            for h, dst in enumerate((to1, to2)):
                for m in range(2):
                    dst[at, m * L : (m + 1) * L] = pbuf[pl.ds(2 * m + h, T, stride=4), :].astype(jnp.bfloat16)

        loop(rows // T, body)

    def send_slopes(e, j):
        pack_slopes(block_row(e, j), s1, s2)
        remote(1, s1, r1, e, j, k).start()

    each_block(send_slopes)
    pack_slopes(block_row(1, k), r1, r2)

    def margin(p, arrived):
        def spread(c):
            b = pl.multiple_of(c * T, T)
            x = arrived[pl.ds(b, T), :].astype(jnp.float32)
            for h in range(2):
                pbuf[pl.ds(h, T, stride=2), :] = x[:, h * L : (h + 1) * L]

            def one(u):
                mtab[b + u] = pbuf[pl.ds(2 * u, 2), :]

            unrolled(T, one)

        loop(arrived.shape[0] // T, spread)

        def split(weight):
            high = weight.astype(jnp.bfloat16)
            low = (weight - high.astype(jnp.float32)).astype(jnp.bfloat16)
            return jnp.concatenate([high, low], axis=0)

        def body(n):
            def one(u):
                gbuf[pl.ds(2 * u, 2), :] = mtab[slot[n * margins + u]]

            unrolled(margins, one)
            tile = pl.ds(n, 1)
            lane = lax.broadcasted_iota(jnp.int32, (1, margins), 1)
            w = jnp.where(lane < count[n], area[tile, :], 0.0)
            hit = lax.broadcasted_iota(jnp.int32, (TT, margins), 0) == cell[tile, :]
            w = jnp.where(hit, w, 0.0)
            total = jnp.sum(w, axis=1, keepdims=True)
            parts = [gbuf[pl.ds(h, margins, stride=2), :].astype(jnp.bfloat16) for h in range(2)]
            at = pl.ds(pl.multiple_of(n * TT, TT), TT)
            if p == 0:
                acc = jnp.dot(split(w), jnp.concatenate(parts, axis=1), preferred_element_type=jnp.float32)
                out[at, :] = (acc[:TT] + acc[TT:]) / total
            else:
                lhs = jnp.concatenate([split(w * offset[0, tile, :]), split(w * offset[1, tile, :])], axis=1)
                acc = jnp.dot(lhs, jnp.concatenate(parts, axis=0), preferred_element_type=jnp.float32)
                lanes = slice((p - 1) * L, p * L)
                out[at, lanes] = out[at, lanes] + (acc[:TT] + acc[TT:]) / total

        loop(tile_count, body)

    receive(0, s0, r0)
    margin(0, r0)
    each_block(lambda e, j: remote(2, s2, r2, e, j, k).start())
    receive(1, s1, r1)
    margin(1, r1)
    receive(2, s2, r2)
    margin(2, r2)
    for copy in halo:
        copy.wait_send()
    for p, src, dst in ((0, s0, r0), (1, s1, r1), (2, s2, r2)):
        each_block(lambda e, j: remote(p, src, dst, e, j, k).wait_send())


def local(
    values,
    halo_rows,
    neighbors,
    grad_weights,
    face_offsets,
    send_rows,
    margin_slot,
    margin_cell,
    margin_count,
    margin_area,
    margin_offset,
):
    regions = lax.axis_size("region")
    tiles = lax.axis_size("tile")
    cells, width = values.shape
    hs = halo_rows.shape[1]
    rows = send_rows.shape[1]
    tile_count, margins = margin_slot.shape
    geom = jnp.concatenate([grad_weights.reshape(12, cells), face_offsets.reshape(12, cells)], axis=0).T
    vmem = pl.BlockSpec(memory_space=pltpu.VMEM)
    smem = pl.BlockSpec(memory_space=pltpu.SMEM)
    block = pltpu.VMEM((rows, width), jnp.bfloat16)
    halo = pltpu.VMEM((2 * hs, width), jnp.bfloat16)
    return pl.pallas_call(
        functools.partial(remap_kernel, regions, tiles),
        out_shape=jax.ShapeDtypeStruct((tile_count * TT, width), jnp.float32),
        in_specs=[vmem, vmem, smem, smem, smem, smem, vmem, smem, vmem, vmem],
        out_specs=vmem,
        scratch_shapes=[
            pltpu.VMEM((cells + 2 * hs, 2, L), jnp.float32),
            pltpu.VMEM((2 * 6 * 32, L), jnp.float32),
            pltpu.VMEM((cells, 4, L), jnp.float32),
            pltpu.VMEM((4 * 32, L), jnp.float32),
            halo,
            halo,
            block,
            block,
            block,
            block,
            block,
            block,
            pltpu.VMEM((rows, 2, L), jnp.float32),
            pltpu.VMEM((2 * margins, L), jnp.float32),
            pltpu.SemaphoreType.DMA((2,)),
            pltpu.SemaphoreType.DMA((2,)),
            pltpu.SemaphoreType.DMA((9 * tiles,)),
            pltpu.SemaphoreType.DMA((9 * tiles,)),
        ],
        compiler_params=pltpu.CompilerParams(collective_id=0, has_side_effects=True, vmem_limit_bytes=VMEM_LIMIT),
        name="remap",
    )(
        values,
        geom,
        neighbors.reshape(-1),
        send_rows.reshape(-1),
        halo_rows.reshape(-1),
        margin_slot.reshape(-1),
        margin_cell,
        margin_count,
        margin_area,
        margin_offset,
    )


def solution(mesh):
    return jax.shard_map(
        local,
        mesh=mesh,
        in_specs=(
            P(("region", "tile"), None),
            P(None, ("region", "tile")),
            P(None, ("region", "tile")),
            P(None, None, ("region", "tile")),
            P(None, None, ("region", "tile")),
            P(("region", "tile"), None),
            P(("region", "tile"), None),
            P(("region", "tile"), None),
            P(("region", "tile")),
            P(("region", "tile"), None),
            P(None, ("region", "tile"), None),
        ),
        out_specs=P(("region", "tile"), None),
        check_vma=False,
    )
```

```python
import functools

import jax
import jax.numpy as jnp
from jax import lax
from jax.experimental import pallas as pl
from jax.experimental.pallas import tpu as pltpu
from jax.sharding import PartitionSpec as P

TT = 32
EPS = 0.04
MESH = pl.DeviceIdType.MESH
L = 128
VMEM_LIMIT = 60 * 1024 * 1024


def limit_block(center, beside, geom):
    grad_x = None
    upper = center
    lower = center
    for j in range(6):
        diff = beside[j] - center
        px = geom(j) * diff
        py = geom(6 + j) * diff
        grad_x = px if grad_x is None else grad_x + px
        grad_y = py if j == 0 else grad_y + py
        upper = jnp.maximum(upper, beside[j])
        lower = jnp.minimum(lower, beside[j])
    head = upper - center
    foot = lower - center
    head2 = head * head + EPS
    foot2 = foot * foot + EPS
    num = None
    for j in range(6):
        delta = grad_x * geom(12 + j) + grad_y * geom(18 + j)
        up = delta > 0
        bound = jnp.where(up, head, foot)
        s = jnp.where(up, head2, foot2)
        p = delta * bound
        sp = s + p
        n = sp + p
        d = sp + 2.0 * (delta * delta)
        if num is None:
            less = n < d
            num = jnp.where(less, n, 1.0)
            den = jnp.where(less, d, 1.0)
        else:
            less = n * den < num * d
            num = jnp.where(less, n, num)
            den = jnp.where(less, d, den)
    lim = num / den
    return lim * grad_x, lim * grad_y


def loop(count, body):
    def step(c, carry):
        body(c)
        return carry

    lax.fori_loop(0, count, step, 0)


def unrolled(count, body):
    def step(c, carry):
        body(c)
        return carry

    lax.fori_loop(0, count, step, 0, unroll=True)


def remap_kernel(
    regions, tiles, vals, weights, faces, nb, send, listed, slot, cell, count, area, offset, out,
    tab, nbuf, rec, pbuf, hsend, hrecv, s0, s1, s2, r0, r1, r2, mtab, gbuf, gstack, geom,
    hsend_sem, hrecv_sem, send_sem, recv_sem,
):
    g = lax.axis_index("region")
    k = lax.axis_index("tile")
    devices = regions * tiles
    me = g * tiles + k
    cells = vals.shape[0]
    hs = hsend.shape[0] // 2
    rows = s0.shape[0] // (3 * tiles)
    tile_count, margins = cell.shape
    T = 32
    C = 128
    G = gbuf.shape[0] // (2 * margins)

    barrier = pltpu.get_barrier_semaphore()
    partners = 0
    for step in (-1, 0, 1):
        for d in range(tiles):
            if step == 0 and d == 0:
                continue
            where = (lax.rem(g + step + regions, regions), lax.rem(k + d, tiles))
            pl.semaphore_signal(barrier, inc=1, device_id=where, device_id_type=MESH)
            partners += 1

    def spread(src, b, dst, start):
        for v in range(0, C, T):
            x = src[pl.ds(b + v, T), :].astype(jnp.float32)
            for h in range(2):
                pbuf[pl.ds(2 * v + h, T, stride=2), :] = x[:, h * L : (h + 1) * L]

            def one(u):
                dst[start + b + v + u] = pbuf[pl.ds(2 * (v + u), 2), :]

            unrolled(T, one)

    def fill(src, start):
        loop(src.shape[0] // C, lambda c: spread(src, pl.multiple_of(c * C, C), tab, start))

    fill(vals, 0)
    pl.semaphore_wait(barrier, partners)

    def pack_values(index, src_row, dst, dst_row, n):
        def body(c):
            b = pl.multiple_of(c * C, C)
            for v in range(0, C, T):

                def one(u):
                    pbuf[pl.ds(2 * (v + u), 2), :] = tab[index(src_row + b + v + u)]

                unrolled(T, one)
                at = pl.ds(pl.multiple_of(dst_row + b, C) + v, T)
                for h in range(2):
                    dst[at, h * L : (h + 1) * L] = pbuf[pl.ds(2 * v + h, T, stride=2), :].astype(jnp.bfloat16)

        loop(n // C, body)

    for part in range(2):
        pack_values(lambda r: listed[part, r], 0, hsend, part * hs, hs)
    halo = []
    for part, step in ((1, 1), (0, devices - 1)):
        to = lax.rem(me + step, devices)
        copy = pltpu.make_async_remote_copy(
            src_ref=hsend.at[pl.ds(part * hs, hs), :],
            dst_ref=hrecv.at[pl.ds((1 - part) * hs, hs), :],
            send_sem=hsend_sem.at[part],
            recv_sem=hrecv_sem.at[part],
            device_id=(to // tiles, lax.rem(to, tiles)),
            device_id_type=MESH,
        )
        copy.start()
        halo.append(copy)

    def block_row(e, j):
        return pl.multiple_of((e * tiles + j) * rows, rows)

    def remote(p, src, dst, e, j, at):
        return pltpu.make_async_remote_copy(
            src_ref=src.at[pl.ds(block_row(e, j), rows), :],
            dst_ref=dst.at[pl.ds(block_row(e, at), rows), :],
            send_sem=send_sem.at[p * 3 * tiles + e * tiles + j],
            recv_sem=recv_sem.at[p * 3 * tiles + e * tiles + at],
            device_id=(lax.rem(g + 1 - e + regions, regions), j),
            device_id_type=MESH,
        )

    def each_block(body):
        def far(d):
            j = lax.rem(k + d, tiles)
            body(0, j)
            body(2, j)

        loop(tiles, far)
        loop(tiles - 1, lambda d: body(1, lax.rem(k + d + 1, tiles)))

    def receive(p, src, dst):
        def far(d):
            j = lax.rem(k + d, tiles)
            remote(p, src, dst, 0, j, j).wait_recv()
            remote(p, src, dst, 2, j, j).wait_recv()

        def near(d):
            j = lax.rem(k + d + 1, tiles)
            remote(p, src, dst, 1, j, j).wait_recv()

        loop(tiles, far)
        loop(tiles - 1, near)

    def send_values(e, j):
        row = block_row(e, j)
        pack_values(lambda r: send[0, r], row, s0, row, rows)
        remote(0, s0, r0, e, j, k).start()

    each_block(send_values)
    pack_values(lambda r: send[0, r], block_row(1, k), r0, block_row(1, k), rows)

    for copy in halo:
        copy.wait_recv()
    fill(hrecv, cells)

    gstack[...] = jnp.zeros_like(gstack)

    def source_chunk(o):
        chunk = pl.multiple_of(o * C, C)
        for m in range(2):
            gstack[8 * m : 8 * m + 6, :] = weights[m, :, pl.ds(chunk, C)]
            gstack[16 + 8 * m : 22 + 8 * m, :] = faces[m, :, pl.ds(chunk, C)]
        geom[...] = gstack[...].T

        def source(c):
            t = pl.multiple_of(c * T, T)
            b = pl.multiple_of(chunk + t, T)
            mine = vals[pl.ds(b, T), :].astype(jnp.float32)
            for s in range(T // 8):

                def gather(q):
                    j = q // 8
                    u = 8 * s + q % 8
                    nbuf[pl.ds(2 * (48 * s + q), 2), :] = tab[nb[j, b + u]]

                for q in range(48):
                    gather(q)
                w = geom[pl.ds(t + 8 * s, 8), :]
                cols = [jnp.broadcast_to(w[:, m : m + 1], (8, L)) for m in range(32)]
                for h in range(2):
                    center = mine[8 * s : 8 * s + 8, h * L : (h + 1) * L]
                    beside = [nbuf[pl.ds(2 * (48 * s + 8 * j) + h, 8, stride=2), :] for j in range(6)]
                    gx, gy = limit_block(center, beside, lambda m: cols[m + 2 * (m // 6)])
                    pbuf[pl.ds(32 * s + h, 8, stride=4), :] = gx
                    pbuf[pl.ds(32 * s + 2 + h, 8, stride=4), :] = gy
                for u in range(8 * s, 8 * s + 8):
                    rec[b + u] = pbuf[pl.ds(4 * u, 4), :]

        loop(C // T, source)

    loop(cells // C, source_chunk)

    def pack_slopes(src_row, to1, to2):
        def body(c):
            b = pl.multiple_of(c * C, C)
            for v in range(0, C, T):

                def one(u):
                    pbuf[pl.ds(4 * (v + u), 4), :] = rec[send[0, src_row + b + v + u]]

                unrolled(T, one)
                at = pl.ds(pl.multiple_of(src_row + b, C) + v, T)
                for h, dst in enumerate((to1, to2)):
                    for m in range(2):
                        x = pbuf[pl.ds(4 * v + 2 * m + h, T, stride=4), :]
                        dst[at, m * L : (m + 1) * L] = x.astype(jnp.bfloat16)

        loop(rows // C, body)

    def send_slopes(e, j):
        pack_slopes(block_row(e, j), s1, s2)
        remote(1, s1, r1, e, j, k).start()

    each_block(send_slopes)
    pack_slopes(block_row(1, k), r1, r2)

    def margin(p, arrived):
        loop(arrived.shape[0] // C, lambda c: spread(arrived, pl.multiple_of(c * C, C), mtab, 0))

        def split(weight):
            high = weight.astype(jnp.bfloat16)
            low = (weight - high.astype(jnp.float32)).astype(jnp.bfloat16)
            return jnp.concatenate([high, low], axis=0)

        def tile_sums(n, v):
            base = 2 * margins * v

            def one(u):
                gbuf[pl.ds(base + 2 * u, 2), :] = mtab[slot[n, u]]

            unrolled(margins, one)
            tile = pl.ds(n, 1)
            lane = lax.broadcasted_iota(jnp.int32, (1, margins), 1)
            w = jnp.where(lane < count[n], area[tile, :], 0.0)
            hit = lax.broadcasted_iota(jnp.int32, (TT, margins), 0) == cell[tile, :]
            w = jnp.where(hit, w, 0.0)
            total = jnp.sum(w, axis=1, keepdims=True)
            parts = [gbuf[pl.ds(base + h, margins, stride=2), :].astype(jnp.bfloat16) for h in range(2)]
            at = pl.ds(pl.multiple_of(n * TT, TT), TT)
            if p == 0:
                acc = jnp.dot(split(w), jnp.concatenate(parts, axis=1), preferred_element_type=jnp.float32)
                out[at, :] = (acc[:TT] + acc[TT:]) / total
            else:
                lhs = jnp.concatenate([split(w * offset[0, tile, :]), split(w * offset[1, tile, :])], axis=1)
                acc = jnp.dot(lhs, jnp.concatenate(parts, axis=0), preferred_element_type=jnp.float32)
                lanes = slice((p - 1) * L, p * L)
                out[at, lanes] = out[at, lanes] + (acc[:TT] + acc[TT:]) / total

        def body(c):
            for v in range(G):
                tile_sums(c * G + v, v)

        loop(tile_count // G, body)

    receive(0, s0, r0)
    margin(0, r0)
    each_block(lambda e, j: remote(2, s2, r2, e, j, k).start())
    receive(1, s1, r1)
    margin(1, r1)
    receive(2, s2, r2)
    margin(2, r2)
    for copy in halo:
        copy.wait_send()
    for p, src, dst in ((0, s0, r0), (1, s1, r1), (2, s2, r2)):
        each_block(lambda e, j: remote(p, src, dst, e, j, k).wait_send())


def local(
    values,
    halo_rows,
    neighbors,
    grad_weights,
    face_offsets,
    send_rows,
    margin_slot,
    margin_cell,
    margin_count,
    margin_area,
    margin_offset,
):
    regions = lax.axis_size("region")
    tiles = lax.axis_size("tile")
    cells, width = values.shape
    hs = halo_rows.shape[1]
    rows = send_rows.shape[1]
    tile_count, margins = margin_slot.shape
    group = 4 if tile_count % 4 == 0 else 1
    vmem = pl.BlockSpec(memory_space=pltpu.VMEM)
    smem = pl.BlockSpec(memory_space=pltpu.SMEM)
    block = pltpu.VMEM((rows, width), jnp.bfloat16)
    halo = pltpu.VMEM((2 * hs, width), jnp.bfloat16)
    return pl.pallas_call(
        functools.partial(remap_kernel, regions, tiles),
        out_shape=jax.ShapeDtypeStruct((tile_count * TT, width), jnp.float32),
        in_specs=[vmem, vmem, vmem, smem, smem, smem, smem, vmem, smem, vmem, vmem],
        out_specs=vmem,
        scratch_shapes=[
            pltpu.VMEM((cells + 2 * hs, 2, L), jnp.float32),
            pltpu.VMEM((2 * 6 * 32, L), jnp.float32),
            pltpu.VMEM((cells, 4, L), jnp.float32),
            pltpu.VMEM((4 * 128, L), jnp.float32),
            halo,
            halo,
            block,
            block,
            block,
            block,
            block,
            block,
            pltpu.VMEM((rows, 2, L), jnp.float32),
            pltpu.VMEM((2 * margins * group, L), jnp.float32),
            pltpu.VMEM((32, 128), jnp.float32),
            pltpu.VMEM((128, 32), jnp.float32),
            pltpu.SemaphoreType.DMA((2,)),
            pltpu.SemaphoreType.DMA((2,)),
            pltpu.SemaphoreType.DMA((9 * tiles,)),
            pltpu.SemaphoreType.DMA((9 * tiles,)),
        ],
        compiler_params=pltpu.CompilerParams(collective_id=0, has_side_effects=True, vmem_limit_bytes=VMEM_LIMIT),
        name="remap",
    )(
        values,
        grad_weights,
        face_offsets,
        neighbors,
        send_rows,
        halo_rows,
        margin_slot,
        margin_cell,
        margin_count,
        margin_area,
        margin_offset,
    )


def solution(mesh):
    return jax.shard_map(
        local,
        mesh=mesh,
        in_specs=(
            P(("region", "tile"), None),
            P(None, ("region", "tile")),
            P(None, ("region", "tile")),
            P(None, None, ("region", "tile")),
            P(None, None, ("region", "tile")),
            P(("region", "tile"), None),
            P(("region", "tile"), None),
            P(("region", "tile"), None),
            P(("region", "tile")),
            P(("region", "tile"), None),
            P(None, ("region", "tile"), None),
        ),
        out_specs=P(("region", "tile"), None),
        check_vma=False,
    )
```
